32 devices in a mesh: row: 8 (over z, x), col: 4 (over y, core).
Axes of the slice: x: 2, y: 2, z: 4, core: 2. Of those that a mesh axis runs over, the one named last changes fastest.
Arguments:
- density: float32 [10240, 10240], P('row', 'col'), may hold values from -6 to 6
- core_hamiltonian: float32 [10240, 10240], P('row', 'col'), may hold values from -6 to 6
- class_tables: float32 [4, 256, 256], replicated, may hold values from -0.375 to 0.375
- shell_scale: float32 [10240], replicated, may hold values from 0.5 to 1.5
- block_place: int32 [640], replicated, may hold values from 0 to 639, as said below
- work_blocks: int32 [32, 32], P(('row', 'col')), may hold values from 0 to 639, as said below
- quartet_bra: int32 [32, 512], P(('row', 'col')), may hold values from 0 to 1023
- quartet_ket: int32 [32, 512], P(('row', 'col')), may hold values from 0 to 1023
- quartet_class: int32 [32, 512], P(('row', 'col')), may hold values from 0 to 3
- quartet_factor: float32 [32, 512], P(('row', 'col')), may hold values from 0.25 to 1
- quartet_count: int32 [32], P(('row', 'col')), may hold values from 1 to 512, 5120 in all
Outputs:
- fock_matrix: float32 [10240, 10240], P('row', 'col')
The draws below stay inside these ranges and needn't reach their ends.
Inputs may be any that keep to these rules, and one draw needn't show every extreme that they name: `block_place`: a permutation of the 640 shell blocks. `work_blocks`: each device's 32 shell blocks are distinct and listed in increasing block_place; exactly 4 of them have places in each run of 80 = 80 consecutive places from 0 (one block row of devices), and likewise exactly 8 in each run of 40 = 160 (one block column of devices).
All inputs are finite; a program needn't handle non-finite values. No bound on the sum of `quartet_count` on one device may be relied on, other than what follows from the above.
Results may differ from the reference program's by a relative error of at most 0.0003.
Values sent between devices are 32-bit elements; how exact they have to be, the bound alone decides.
A program may use at most 320 MiB of HBM per device.

```python
import math
import jax
import jax.numpy as jnp
import numpy as np
from jax import lax

SHELL = 16
PAIRS = 256
NBF = 10240
NFB = 640
ROW_SHELLS = 80
COL_SHELLS = 160
WORK = 32
CLASSES = 4
QMAX = 512
QAVG = 160
DEVICES = 32


def place_order(key):
    return jax.random.permutation(jax.random.fold_in(key, 91), NFB).astype(jnp.int32)


def draw_block_place(key, part):
    return place_order(key)


def draw_work_blocks(key, part):
    places = place_order(key)
    key = jax.random.fold_in(key, 3)
    stripe = min(ROW_SHELLS, COL_SHELLS)
    stripes = NFB // stripe
    chosen = WORK // stripes
    scores = jax.random.randint(key, (DEVICES, stripes, stripe), 0, 2 ** 30)
    ranked = jnp.sort(jnp.argsort(scores, axis=-1)[..., :chosen], axis=-1)
    positions = ranked + stripe * jnp.arange(stripes)[None, :, None]
    inverse = jnp.argsort(places)
    return inverse[positions.reshape(DEVICES, WORK)].astype(jnp.int32)


def with_ends(drawn, own_key, low, high):
    shape = drawn.shape
    place = [jax.random.randint(jax.random.fold_in(own_key, axis), (), 0, shape[axis]) for axis in range(len(shape))]
    drawn = drawn.at[tuple(place)].set(low)
    longest = shape.index(max(shape))
    place[longest] = (place[longest] + 1) % shape[longest]
    return drawn.at[tuple(place)].set(high)


def steps_of(key, dims, shards, least, largest):
    level, own = 1.0, jax.random.fold_in(key, 6)
    for dim, blocks in shards:
        draws = jnp.exp(jax.random.uniform(jax.random.fold_in(own, dim), (blocks,), jnp.float32, least / len(shards), largest / len(shards)))
        level = level * jnp.repeat(draws, dims[dim] // blocks).reshape([-1 if axis == dim else 1 for axis in range(len(dims))])
    return level


def length_profile(count, total, most, skew):
    loads = [(1 << 20) // math.isqrt(standing ** skew) + 1 for standing in range(2, count + 1)]
    surplus, counts = total - most - (count - 1), [1] * (count - 1)
    while surplus > 0:
        candidates = [i for i in range(count - 1) if counts[i] < most]
        whole, budget = sum([loads[i] for i in candidates]), surplus
        for i in candidates:
            addition = min(most - counts[i], max(1, budget * loads[i] // whole), surplus)
            counts[i] = counts[i] + addition
            surplus = surplus - addition
    return np.array([most] + counts)


def uneven_parts(key, number_of, total, most, slope):
    if number_of == 2:
        one = jax.random.randint(key, (), max(1, total - most), min(most, total - 1) + 1)
        return jnp.stack([one, total - one])
    lengths = jnp.asarray(length_profile(number_of, total, most, slope), jnp.int32)
    twos = (number_of - 1) // 2
    giver, taker = lengths[1:1 + 2 * twos:2], lengths[2:2 + 2 * twos:2]
    room = jnp.minimum(giver - 1, most - taker)
    shifted = jax.random.randint(jax.random.fold_in(key, 1), (twos,), 0, 1 << 20) % (room + 1)
    lengths = lengths.at[1:1 + 2 * twos:2].set(giver - shifted).at[2:2 + 2 * twos:2].set(taker + shifted)
    return lengths[jax.random.permutation(jax.random.fold_in(key, 2), number_of)]


def noise(key, dims, deviation, most, shards=(), dtype=jnp.bfloat16):
    loudness = steps_of(key, dims, shards, -0.22, 0.18) if shards else 1.0
    values = jax.random.normal(key, dims, jnp.float32) * deviation * loudness
    return jnp.minimum(jnp.maximum(values, -most), most).astype(dtype)


def setup_inputs(seed: int = 0) -> dict:
    splits = jax.random.split(jax.random.key(seed), 12)
    density = noise(splits[0], (NBF, NBF), 1.0, 6.0, ((0, 8), (1, 4)), jnp.float32)
    core_hamiltonian = noise(splits[1], (NBF, NBF), 1.0, 6.0, ((0, 8), (1, 4)), jnp.float32)
    class_tables = noise(splits[2], (CLASSES, PAIRS, PAIRS), PAIRS ** -0.5, 0.375, (), jnp.float32)
    shell_scale = jnp.clip(jnp.exp(jax.random.uniform(splits[3], (NBF,), jnp.float32, math.log(0.5), math.log(1.5))), 0.5, 1.5)
    block_place = draw_block_place(jax.random.fold_in(splits[11], 71), 0)
    work_blocks = draw_work_blocks(jax.random.fold_in(splits[11], 71), 0)
    quartet_bra = with_ends(jax.random.randint(splits[6], (DEVICES, QMAX), 0, WORK * WORK), jax.random.fold_in(splits[6], 1), 0, (WORK * WORK) - 1).astype(jnp.int32)
    quartet_ket = with_ends(jax.random.randint(splits[7], (DEVICES, QMAX), 0, WORK * WORK), jax.random.fold_in(splits[7], 1), 0, (WORK * WORK) - 1).astype(jnp.int32)
    quartet_class = with_ends(jax.random.randint(splits[8], (DEVICES, QMAX), 0, CLASSES), jax.random.fold_in(splits[8], 1), 0, CLASSES - 1).astype(jnp.int32)
    quartet_factor = jnp.clip(jnp.exp(math.log(1.0) - 1.3862944 * jax.random.uniform(splits[9], (DEVICES, QMAX), jnp.float32) ** steps_of(splits[9], (DEVICES, QMAX), ((0, 32),), -0.2, 0.2)), 0.25, 1.0)
    quartet_count = uneven_parts(splits[10], DEVICES, QAVG * DEVICES, QMAX, 2).astype(jnp.int32)
    return {"density": density, "core_hamiltonian": core_hamiltonian, "class_tables": class_tables, "shell_scale": shell_scale, "block_place": block_place, "work_blocks": work_blocks, "quartet_bra": quartet_bra, "quartet_ket": quartet_ket, "quartet_class": quartet_class, "quartet_factor": quartet_factor, "quartet_count": quartet_count}


ORDERS = ((3, 4, 0, 1, 2), (1, 2, 0, 3, 4), (2, 4, 0, 1, 3), (1, 3, 0, 2, 4), (2, 3, 0, 1, 4), (1, 4, 0, 2, 3))
COEFFS = (1.0, 1.0, -0.5, -0.5, -0.5, -0.5)


def make_stacks(class_tables):
    classes = class_tables.shape[0]
    pair_width = class_tables.shape[1]
    tensor = class_tables.reshape(classes, SHELL, SHELL, SHELL, SHELL)
    return [jnp.transpose(tensor, layout).reshape(pair_width, classes * pair_width) for layout in ORDERS]


def pair_weights(weights):
    block_count = weights.shape[0]
    shell_width = weights.shape[1]
    outer = weights[:, None, :, None] * weights[None, :, None, :]
    return outer.reshape(block_count * block_count, shell_width * shell_width)


def quartet_terms(scaled, bra_pairs, ket_pairs, klasses, factors, stacks, task_count):
    shell_a = bra_pairs // task_count
    shell_b = bra_pairs % task_count
    shell_c = ket_pairs // task_count
    shell_d = ket_pairs % task_count
    sources = (shell_c * task_count + shell_d, shell_a * task_count + shell_b,
               shell_b * task_count + shell_d, shell_a * task_count + shell_c,
               shell_b * task_count + shell_c, shell_a * task_count + shell_d)
    targets = (sources[1], sources[0], sources[3], sources[2], sources[5], sources[4])
    pair_width = scaled.shape[1]
    classes = stacks[0].shape[1] // pair_width
    select = (klasses[:, None] == jnp.arange(classes)[None, :]).astype(jnp.float32)
    values = []
    for source, table_stack, weighting in zip(sources, stacks, COEFFS):
        product = jnp.dot(scaled[source], table_stack, precision=lax.Precision.HIGHEST)
        product = product.reshape(source.shape[0], classes, pair_width)
        chosen = jnp.sum(product * select[:, :, None], axis=1)
        values.append(chosen * (weighting * factors)[:, None])
    return jnp.concatenate(targets), jnp.concatenate(values)


def reference(density, core_hamiltonian, class_tables, shell_scale, block_place, work_blocks, quartet_bra, quartet_ket, quartet_class, quartet_factor, quartet_count):
    stacks = make_stacks(class_tables)
    density_view = density.reshape(NFB, SHELL, NFB, SHELL)
    scales = shell_scale.reshape(NFB, SHELL)
    slot_index = jnp.arange(QMAX)

    def device_step(totals, items):
        task_list, bra_pairs, ket_pairs, klasses, factors, live_count = items
        places = block_place[task_list]
        blocks = density_view[places[:, None], :, places[None, :], :].reshape(WORK * WORK, PAIRS)
        weights = pair_weights(scales[task_list])
        scaled = blocks * weights
        factors = jnp.where(slot_index < live_count, factors, 0.0)
        targets, values = quartet_terms(scaled, bra_pairs, ket_pairs, klasses, factors, stacks, WORK)
        partial_value = jnp.zeros((WORK * WORK, PAIRS), jnp.float32).at[targets].add(values)
        partial_value = (partial_value * weights).reshape(WORK, WORK, SHELL, SHELL)
        totals = totals.at[places[:, None], :, places[None, :], :].add(partial_value)
        return totals, None

    totals = jnp.zeros((NFB, SHELL, NFB, SHELL), jnp.float32)
    totals = lax.scan(device_step, totals, (work_blocks, quartet_bra, quartet_ket, quartet_class, quartet_factor, quartet_count))[0]
    return core_hamiltonian + totals.reshape(NBF, NBF)
```

```python
import functools

import jax
import jax.numpy as jnp
from jax import lax
from jax.experimental import pallas as pl
from jax.experimental.pallas import tpu as pltpu
from jax.sharding import PartitionSpec as P

SHELL = 16
LANES = 128
GROUP = LANES // SHELL
CHUNK = 128
VMEM_LIMIT = 56 * 1024 * 1024
MESH = pl.DeviceIdType.MESH


def flat_index(cols):
    return lax.axis_index("row") * cols + lax.axis_index("col")


def coords(device, cols):
    return (device // cols, device % cols)


def slot_of(device, rows, cols):
    return (device % cols) * rows + device // cols


def greet_all(me, count, cols):
    barrier = pltpu.get_barrier_semaphore()

    def greet(step, carry):
        pl.semaphore_signal(
            barrier, inc=1, device_id=coords((me + step) % count, cols), device_id_type=MESH
        )
        return carry

    lax.fori_loop(1, count, greet, 0)
    pl.semaphore_wait(barrier, count - 1)


def share_kernel(rows, cols, work_ref, out_ref, send_sem, recv_sem):
    count = rows * cols
    me = flat_index(cols)
    greet_all(me, count, cols)

    def copy(step, slot):
        return pltpu.make_async_remote_copy(
            src_ref=work_ref,
            dst_ref=out_ref.at[slot],
            send_sem=send_sem.at[step],
            recv_sem=recv_sem.at[step],
            device_id=coords((me + step) % count, cols),
            device_id_type=MESH,
        )

    def send(step, carry):
        copy(step, me).start()
        return carry

    def finish(step, carry):
        copy(step, (me - step + count) % count).wait_recv()
        copy(step, me).wait_send()
        return carry

    lax.fori_loop(1, count, send, 0)
    out_ref[me] = work_ref[...]
    lax.fori_loop(1, count, finish, 0)


def exchange_kernel(rows, cols, src_ref, dst_ref, send_sem, recv_sem, own_sem):
    count = rows * cols
    me = flat_index(cols)
    greet_all(me, count, cols)

    def copy(step, slot):
        target = (me + step) % count
        return pltpu.make_async_remote_copy(
            src_ref=src_ref.at[slot_of(target, rows, cols)],
            dst_ref=dst_ref.at[slot],
            send_sem=send_sem.at[step],
            recv_sem=recv_sem.at[step],
            device_id=coords(target, cols),
            device_id_type=MESH,
        )

    own = slot_of(me, rows, cols)

    def send(step, carry):
        copy(step, own).start()
        return carry

    def finish(step, carry):
        copy(step, slot_of((me - step + count) % count, rows, cols)).wait_recv()
        copy(step, own).wait_send()
        return carry

    lax.fori_loop(1, count, send, 0)
    own_copy = pltpu.make_async_copy(src_ref.at[own], dst_ref.at[own], own_sem)
    own_copy.start()
    lax.fori_loop(1, count, finish, 0)
    own_copy.wait()


def lane_granule(rows):
    return lax.broadcasted_iota(jnp.int32, (rows, LANES), 1) // SHELL


def swap_granules(arrays):
    granule = lane_granule(arrays[0].shape[0])
    for distance in (4, 2, 1):
        keep = (granule & distance) == 0
        result = list(arrays)
        for i in range(GROUP):
            if i & distance == 0:
                low, high = arrays[i], arrays[i + distance]
                result[i] = jnp.where(keep, low, pltpu.roll(high, SHELL * distance, 1))
                result[i + distance] = jnp.where(
                    keep, pltpu.roll(low, LANES - SHELL * distance, 1), high
                )
        arrays = result
    return arrays


def places_of(device, place_ref, tasks_ref, row_share, col_share, row_blocks, col_blocks):
    row_base = lax.axis_index("row") * row_share
    col_base = lax.axis_index("col") * col_share
    row_starts, col_starts, col_offsets = [], [], []
    for r in range(row_share):
        place = place_ref[tasks_ref[device, 0, row_base + r]]
        row_starts.append(pl.multiple_of(lax.rem(place, row_blocks) * SHELL, SHELL))
    for k in range(col_share):
        place = lax.rem(place_ref[tasks_ref[device, 0, col_base + k]], col_blocks)
        col_starts.append(pl.multiple_of(lax.div(place, GROUP) * LANES, LANES))
        col_offsets.append(lax.rem(place, GROUP))
    return row_starts, col_starts, col_offsets


def copy_chunks(src_ref, dst_ref, sems):
    parts = sems.shape[0]
    height = dst_ref.shape[0] // parts
    copies = []
    for part in range(parts):
        window = pl.ds(part * height, height)
        pair = (src_ref.at[window], dst_ref.at[window])
        copies.append(pltpu.make_async_copy(pair[0], pair[1], sems.at[part]))
    for copy in copies:
        copy.start()
    for copy in copies:
        copy.wait()


def pack_kernel(
    rows, cols, row_share, col_share, place_ref, tasks_ref, density_ref, out_ref, held, sems
):
    copy_chunks(density_ref, held, sems)
    row_blocks, col_blocks = held.shape[0] // SHELL, held.shape[1] // SHELL
    granule = lane_granule(SHELL)

    def step(slot, carry):
        device = lax.rem(slot, rows) * cols + lax.div(slot, rows)
        row_starts, col_starts, col_offsets = places_of(
            device, place_ref, tasks_ref, row_share, col_share, row_blocks, col_blocks
        )
        slabs = [jnp.zeros((SHELL, LANES), jnp.float32)] * row_share
        for k in range(col_share):
            shift = lax.rem((k + GROUP - col_offsets[k]) * SHELL, LANES)
            for r in range(row_share):
                block = held[pl.ds(row_starts[r], SHELL), pl.ds(col_starts[k], LANES)]
                slabs[r] = jnp.where(granule == k, pltpu.roll(block, shift, 1), slabs[r])
        for r in range(row_share):
            out_ref[slot, pl.ds(r * SHELL, SHELL), :] = slabs[r]
        return carry

    lax.fori_loop(0, rows * cols, step, 0)


def place_kernel(
    rows, cols, row_share, col_share, place_ref, tasks_ref, parts_ref, core_ref, out_ref, held, sems
):
    copy_chunks(core_ref, held, sems)
    row_blocks, col_blocks = held.shape[0] // SHELL, held.shape[1] // SHELL
    granule = lane_granule(SHELL)

    def step(slot, carry):
        device = lax.rem(slot, rows) * cols + lax.div(slot, rows)
        row_starts, col_starts, col_offsets = places_of(
            device, place_ref, tasks_ref, row_share, col_share, row_blocks, col_blocks
        )
        slabs = [parts_ref[slot, pl.ds(r * SHELL, SHELL), :] for r in range(row_share)]
        for k in range(col_share):
            shift = lax.rem((col_offsets[k] + GROUP - k) * SHELL, LANES)
            windows = [
                (pl.ds(row_starts[r], SHELL), pl.ds(col_starts[k], LANES))
                for r in range(row_share)
            ]
            inside = granule == col_offsets[k]
            sums = [
                held[windows[r]] + jnp.where(inside, pltpu.roll(slabs[r], shift, 1), 0.0)
                for r in range(row_share)
            ]
            for r in range(row_share):
                held[windows[r]] = sums[r]
        return carry

    lax.fori_loop(0, rows * cols, step, 0)
    copy_chunks(held, out_ref, sems)


def split_bf16(values):
    high = values.astype(jnp.bfloat16)
    return high, (values - high.astype(jnp.float32)).astype(jnp.bfloat16)


def swap_table(half_ref, stage_ref):
    for a in range(SHELL // GROUP):
        for b in range(SHELL // GROUP):
            arrays = [
                half_ref[b, pl.ds(GROUP * a + i, SHELL, stride=SHELL), :] for i in range(GROUP)
            ]
            for j, array in enumerate(swap_granules(arrays)):
                stage_ref[a, pl.ds(GROUP * b + j, SHELL, stride=SHELL), :] = array


def table_stage(classes, tables_ref, half_ref, stage_ref, tab_ref):
    width = SHELL * SHELL
    row = lax.broadcasted_iota(jnp.int32, (width, width), 0)
    column = lax.broadcasted_iota(jnp.int32, (width, width), 1)
    swap = (row // SHELL == column % SHELL) & (row % SHELL == column // SHELL)
    swap = jnp.where(swap, 1.0, 0.0).astype(jnp.bfloat16)

    def keep(klass, form, values):
        high, low = split_bf16(values)
        tab_ref[klass, form, 0] = high
        tab_ref[klass, form, 1] = low
        return high, low

    def swapped(values):
        for half in range(2):
            half_ref[half] = values[:, half * LANES : (half + 1) * LANES]
        swap_table(half_ref, stage_ref)
        return -0.5 * jnp.concatenate([stage_ref[0], stage_ref[1]], axis=1)

    def step(klass, carry):
        values = tables_ref[klass]
        high, low = keep(klass, 0, values)
        keep(klass, 1, swapped(values))
        permuted = jnp.dot(high, swap, preferred_element_type=jnp.float32)
        permuted = permuted + jnp.dot(low, swap, preferred_element_type=jnp.float32)
        keep(klass, 2, swapped(permuted))
        return carry

    lax.fori_loop(0, classes, step, 0)


def quartet_kernel(
    classes, slots, task_count, col_share,
    work_ref, bra_ref, ket_ref, class_ref, factor_ref, count_ref,
    recv_ref, scale_ref, tables_ref, out_ref,
    half_ref, stage_ref, tab_ref, own_scale, left_ref, right_ref, x_ref, g_ref, y_ref, filled,
):
    width = SHELL * SHELL
    slabs = recv_ref.shape[0] // SHELL
    tiles = slabs // 8
    table_stage(classes, tables_ref, half_ref, stage_ref, tab_ref)

    def scale_step(u, carry):
        shell = work_ref[0, u]
        line = jnp.broadcast_to(scale_ref[pl.ds(lax.div(shell, GROUP), 1), :], (8, LANES))
        shift = lax.rem((GROUP - lax.rem(shell, GROUP)) * SHELL, LANES)
        own_scale[pl.ds(u, 1), :] = pltpu.roll(line, shift, 1)[0:1]
        return carry

    lax.fori_loop(0, task_count, scale_step, 0)
    source = lax.broadcasted_iota(jnp.int32, (LANES, LANES), 0)
    lane = lax.broadcasted_iota(jnp.int32, (LANES, LANES), 1)
    for half in range(2):
        spread = jnp.where(source == lane // SHELL + GROUP * half, 1.0, 0.0)
        left_ref[half] = jnp.dot(own_scale[...], spread, precision=lax.Precision.HIGHEST)
    repeat = jnp.where(source == lane % SHELL, 1.0, 0.0)
    right_ref[...] = jnp.dot(own_scale[...], repeat, precision=lax.Precision.HIGHEST)

    def tile_place(tile):
        u = pl.multiple_of(lax.rem(tile * 8, task_count), 8)
        return u, lax.div(tile * 8, task_count) * col_share

    def spread_step(tile, carry):
        u, v = tile_place(tile)
        for half in range(2):
            arrays = [
                recv_ref[pl.ds(tile * 8 * SHELL + GROUP * half + i, 8, stride=SHELL), :]
                for i in range(GROUP)
            ]
            arrays = swap_granules(arrays)
            left = left_ref[half, pl.ds(u, 8), :]
            for c in range(col_share):
                weight = left * right_ref[pl.ds(v + c, 1), :]
                x_ref[half, pl.ds(pl.multiple_of(c * slabs + tile * 8, 8), 8), :] = arrays[c] * weight
        return carry

    lax.fori_loop(0, tiles, spread_step, 0)

    def zero_step(tile, carry):
        for form in range(6):
            for half in range(2):
                y_ref[form, half, pl.ds(pl.multiple_of(tile * 8, 8), 8), :] = jnp.zeros(
                    (8, LANES), jnp.float32
                )
        return carry

    lax.fori_loop(0, tiles * col_share, zero_step, 0)
    for klass in range(classes):
        filled[klass] = 0

    def pairs_of(n):
        bra, ket = bra_ref[0, n], ket_ref[0, n]
        a, b = lax.div(bra, task_count), lax.rem(bra, task_count)
        c, d = lax.div(ket, task_count), lax.rem(ket, task_count)

        def at(v):
            return lax.rem(v, col_share) * slabs + lax.div(v, col_share) * task_count

        at_c, at_d = at(c), at(d)
        return c + at_d, a + at(b), b + at_d, a + at_c, b + at_c, a + at_d

    live = count_ref[0]

    def gather_step(n, carry):
        klass = class_ref[0, n]
        order = filled[klass]
        filled[klass] = order + 1
        row = klass * slots + order
        factor = factor_ref[0, n]
        sources = pairs_of(n)
        values = [
            [x_ref[half, pl.ds(sources[form], 1), :] * factor for half in range(2)]
            for form in range(6)
        ]
        for form in range(6):
            for half in range(2):
                g_ref[form, half, pl.ds(row, 1), :] = values[form][half]
        return carry

    lax.fori_loop(0, live, gather_step, 0)

    def class_step(klass, carry):
        def chunk_step(chunk, carry):
            rows = pl.ds(pl.multiple_of(klass * slots + chunk * CHUNK, CHUNK), CHUNK)
            for form in range(6):
                table_high = tab_ref[klass, form // 2, 0]
                table_low = tab_ref[klass, form // 2, 1]
                values = jnp.concatenate([g_ref[form, 0, rows, :], g_ref[form, 1, rows, :]], axis=1)
                high, low = split_bf16(values)
                dims = (((1,), (1 if form % 2 == 0 else 0,)), ((), ()))
                product = functools.partial(
                    lax.dot_general, dimension_numbers=dims, preferred_element_type=jnp.float32
                )
                result = product(high, table_high) + product(low, table_high)
                result = result + product(high, table_low)
                g_ref[form, 0, rows, :] = result[:, :LANES]
                g_ref[form, 1, rows, :] = result[:, LANES:]
            return carry

        return lax.fori_loop(0, lax.div(filled[klass] + CHUNK - 1, CHUNK), chunk_step, carry)

    lax.fori_loop(0, classes, class_step, 0)
    for klass in range(classes):
        filled[klass] = 0

    def scatter_step(n, carry):
        klass = class_ref[0, n]
        order = filled[klass]
        filled[klass] = order + 1
        row = klass * slots + order
        pairs = pairs_of(n)
        targets = (pairs[1], pairs[0], pairs[3], pairs[2], pairs[5], pairs[4])
        values = [
            [
                y_ref[form, half, pl.ds(targets[form], 1), :] + g_ref[form, half, pl.ds(row, 1), :]
                for half in range(2)
            ]
            for form in range(6)
        ]
        for form in range(6):
            for half in range(2):
                y_ref[form, half, pl.ds(targets[form], 1), :] = values[form][half]
        return carry

    lax.fori_loop(0, live, scatter_step, 0)

    def collect_step(tile, carry):
        u, v = tile_place(tile)
        for half in range(2):
            left = left_ref[half, pl.ds(u, 8), :]
            arrays = []
            for c in range(GROUP):
                if c < col_share:
                    window = pl.ds(pl.multiple_of(c * slabs + tile * 8, 8), 8)
                    total = y_ref[0, half, window, :]
                    for form in range(1, 6):
                        total = total + y_ref[form, half, window, :]
                    arrays.append(total * (left * right_ref[pl.ds(v + c, 1), :]))
                else:
                    arrays.append(jnp.zeros((8, LANES), jnp.float32))
            for i, array in enumerate(swap_granules(arrays)):
                out_ref[pl.ds(tile * 8 * SHELL + GROUP * half + i, 8, stride=SHELL), :] = array
        return carry

    lax.fori_loop(0, tiles, collect_step, 0)


def on_device(
    density,
    core_hamiltonian,
    class_tables,
    shell_scale,
    block_place,
    work_blocks,
    quartet_bra,
    quartet_ket,
    quartet_class,
    quartet_factor,
    quartet_count,
):
    rows = lax.axis_size("row")
    cols = lax.axis_size("col")
    count = rows * cols
    task_count = work_blocks.shape[1]
    row_share = task_count // rows
    col_share = task_count // cols
    classes = class_tables.shape[0]
    width = class_tables.shape[1]
    slots = quartet_bra.shape[1]
    message = (row_share * SHELL, LANES)
    messages = jax.ShapeDtypeStruct((count,) + message, jnp.float32)
    slab_rows = count * row_share * SHELL
    pair_rows = task_count * task_count

    vmem = pl.BlockSpec(memory_space=pltpu.VMEM)
    smem = pl.BlockSpec(memory_space=pltpu.SMEM)
    hbm = pl.BlockSpec(memory_space=pl.ANY)
    local = pltpu.CompilerParams(vmem_limit_bytes=VMEM_LIMIT)
    parts = 8

    def talk(collective_id):
        return pltpu.CompilerParams(collective_id=collective_id, has_side_effects=True)

    padded = jnp.pad(work_blocks, ((0, 0), (0, LANES - task_count)))
    tasks = pl.pallas_call(
        functools.partial(share_kernel, rows, cols),
        out_shape=jax.ShapeDtypeStruct((count, 1, LANES), jnp.int32),
        in_specs=[vmem],
        out_specs=vmem,
        scratch_shapes=[pltpu.SemaphoreType.DMA((count,)), pltpu.SemaphoreType.DMA((count,))],
        compiler_params=talk(0),
        name="share_tasks",
    )(padded)

    def exchange(collective_id, name, values):
        return pl.pallas_call(
            functools.partial(exchange_kernel, rows, cols),
            out_shape=messages,
            in_specs=[hbm],
            out_specs=hbm,
            scratch_shapes=[
                pltpu.SemaphoreType.DMA((count,)),
                pltpu.SemaphoreType.DMA((count,)),
                pltpu.SemaphoreType.DMA,
            ],
            compiler_params=talk(collective_id),
            name=name,
        )(values)

    sizes = (rows, cols, row_share, col_share)
    picked = pl.pallas_call(
        functools.partial(pack_kernel, *sizes),
        out_shape=messages,
        in_specs=[smem, smem, hbm],
        out_specs=vmem,
        scratch_shapes=[
            pltpu.VMEM(density.shape, jnp.float32),
            pltpu.SemaphoreType.DMA((parts,)),
        ],
        compiler_params=local,
        name="pack_density",
    )(block_place, tasks, density)
    fetched = exchange(1, "fetch_density", picked)

    terms = pl.pallas_call(
        functools.partial(quartet_kernel, classes, slots, task_count, col_share),
        out_shape=jax.ShapeDtypeStruct((slab_rows, LANES), jnp.float32),
        in_specs=[smem] * 6 + [vmem] * 3,
        out_specs=vmem,
        scratch_shapes=[
            pltpu.VMEM((2, width, LANES), jnp.float32),
            pltpu.VMEM((2, width, LANES), jnp.float32),
            pltpu.VMEM((classes, 3, 2, width, width), jnp.bfloat16),
            pltpu.VMEM((task_count, LANES), jnp.float32),
            pltpu.VMEM((2, task_count, LANES), jnp.float32),
            pltpu.VMEM((task_count, LANES), jnp.float32),
            pltpu.VMEM((2, pair_rows, LANES), jnp.float32),
            pltpu.VMEM((6, 2, classes * slots, LANES), jnp.float32),
            pltpu.VMEM((6, 2, pair_rows, LANES), jnp.float32),
            pltpu.SMEM((classes,), jnp.int32),
        ],
        compiler_params=local,
        name="quartets",
    )(
        work_blocks, quartet_bra, quartet_ket, quartet_class, quartet_factor, quartet_count,
        fetched.reshape(slab_rows, LANES),
        shell_scale.reshape(-1, LANES),
        class_tables,
    )
    returned = exchange(2, "return_fock", terms.reshape(messages.shape))

    return pl.pallas_call(
        functools.partial(place_kernel, *sizes),
        out_shape=jax.ShapeDtypeStruct(density.shape, jnp.float32),
        in_specs=[smem, smem, vmem, hbm],
        out_specs=hbm,
        scratch_shapes=[
            pltpu.VMEM(density.shape, jnp.float32),
            pltpu.SemaphoreType.DMA((parts,)),
        ],
        compiler_params=local,
        name="place_fock",
    )(block_place, tasks, returned, core_hamiltonian)


def solution(mesh):
    placed = (
        P("row", "col"),
        P("row", "col"),
        P(),
        P(),
        P(),
        P(("row", "col"), None),
        P(("row", "col"), None),
        P(("row", "col"), None),
        P(("row", "col"), None),
        P(("row", "col"), None),
        P(("row", "col")),
    )
    return jax.shard_map(
        on_device, mesh=mesh, in_specs=placed, out_specs=P("row", "col"), check_vma=False
    )
```

```python
import functools

import jax
import jax.numpy as jnp
from jax import lax
from jax.experimental import pallas as pl
from jax.experimental.pallas import tpu as pltpu
from jax.sharding import PartitionSpec as P

SHELL = 16
LANES = 128
GROUP = LANES // SHELL
CHUNK = 128
VMEM_LIMIT = 56 * 1024 * 1024
PACK_LIMIT = 24 * 1024 * 1024
QUARTET_LIMIT = 36 * 1024 * 1024
SMALL_LIMIT = 4 * 1024 * 1024
MESH = pl.DeviceIdType.MESH


def flat_index(cols):
    return lax.axis_index("row") * cols + lax.axis_index("col")


def coords(device, cols):
    return (device // cols, device % cols)


def slot_of(device, rows, cols):
    return (device % cols) * rows + device // cols


def greet_all(me, count, cols):
    barrier = pltpu.get_barrier_semaphore()

    def greet(step, carry):
        pl.semaphore_signal(
            barrier, inc=1, device_id=coords((me + step) % count, cols), device_id_type=MESH
        )
        return carry

    lax.fori_loop(1, count, greet, 0)
    pl.semaphore_wait(barrier, count - 1)


def share_kernel(rows, cols, task_count, work_ref, out_ref, line_ref, send_sem, recv_sem):
    count = rows * cols
    me = flat_index(cols)
    line_ref[...] = jnp.zeros_like(line_ref)
    line_ref[:, 0:task_count] = work_ref[...]
    greet_all(me, count, cols)

    def copy(step, slot):
        return pltpu.make_async_remote_copy(
            src_ref=line_ref,
            dst_ref=out_ref.at[slot],
            send_sem=send_sem.at[step],
            recv_sem=recv_sem.at[step],
            device_id=coords((me + step) % count, cols),
            device_id_type=MESH,
        )

    def send(step, carry):
        copy(step, me).start()
        return carry

    def finish(step, carry):
        copy(step, (me - step + count) % count).wait_recv()
        copy(step, me).wait_send()
        return carry

    lax.fori_loop(1, count, send, 0)
    out_ref[me] = line_ref[...]
    lax.fori_loop(1, count, finish, 0)


def exchange_kernel(rows, cols, src_ref, dst_ref, send_sem, recv_sem, own_sem, beside=None):
    count = rows * cols
    me = flat_index(cols)
    greet_all(me, count, cols)

    def copy(step, slot):
        target = (me + step) % count
        return pltpu.make_async_remote_copy(
            src_ref=src_ref.at[slot_of(target, rows, cols)],
            dst_ref=dst_ref.at[slot],
            send_sem=send_sem.at[step],
            recv_sem=recv_sem.at[step],
            device_id=coords(target, cols),
            device_id_type=MESH,
        )

    own = slot_of(me, rows, cols)

    def send(step, carry):
        copy(step, own).start()
        return carry

    def finish(step, carry):
        copy(step, slot_of((me - step + count) % count, rows, cols)).wait_recv()
        copy(step, own).wait_send()
        return carry

    lax.fori_loop(1, count, send, 0)
    own_copy = pltpu.make_async_copy(src_ref.at[own], dst_ref.at[own], own_sem)
    own_copy.start()
    if beside is not None:
        beside()
    lax.fori_loop(1, count, finish, 0)
    own_copy.wait()


def lane_granule(rows):
    return lax.broadcasted_iota(jnp.int32, (rows, LANES), 1) // SHELL


def swap_granules(arrays):
    granule = lane_granule(arrays[0].shape[0])
    for distance in (4, 2, 1):
        keep = (granule & distance) == 0
        result = list(arrays)
        for i in range(GROUP):
            if i & distance == 0:
                low, high = arrays[i], arrays[i + distance]
                result[i] = jnp.where(keep, low, pltpu.roll(high, SHELL * distance, 1))
                result[i + distance] = jnp.where(
                    keep, pltpu.roll(low, LANES - SHELL * distance, 1), high
                )
        arrays = result
    return arrays


def places_of(device, place_ref, tasks_ref, row_share, col_share, row_blocks, col_blocks):
    row, col = lax.axis_index("row"), lax.axis_index("col")
    row_starts, col_starts, col_offsets = [], [], []
    for r in range(row_share):
        place = place_ref[tasks_ref[device, 0, row * row_share + r]] - row * row_blocks
        row_starts.append(pl.multiple_of(place * SHELL, SHELL))
    for k in range(col_share):
        place = place_ref[tasks_ref[device, 0, col * col_share + k]] - col * col_blocks
        offset = place & (GROUP - 1)
        col_starts.append(pl.multiple_of((place - offset) * SHELL, LANES))
        col_offsets.append(offset)
    return row_starts, col_starts, col_offsets


def chunk_copies(src_ref, dst_ref, sems):
    parts = sems.shape[0]
    height = dst_ref.shape[0] // parts
    windows = [pl.ds(part * height, height) for part in range(parts)]
    return [
        pltpu.make_async_copy(src_ref.at[window], dst_ref.at[window], sems.at[part])
        for part, window in enumerate(windows)
    ]


def copy_chunks(src_ref, dst_ref, sems):
    copies = chunk_copies(src_ref, dst_ref, sems)
    for copy in copies:
        copy.start()
    for copy in copies:
        copy.wait()


def place_kernel(
    rows, cols, row_share, col_share, place_ref, tasks_ref, parts_ref, core_ref, out_ref, held, sems
):
    copy_chunks(core_ref, held, sems)
    row_blocks, col_blocks = held.shape[0] // SHELL, held.shape[1] // SHELL
    granule = lane_granule(SHELL)

    def step(slot, carry):
        device = lax.rem(slot, rows) * cols + lax.div(slot, rows)
        row_starts, col_starts, col_offsets = places_of(
            device, place_ref, tasks_ref, row_share, col_share, row_blocks, col_blocks
        )
        slabs = [parts_ref[slot, pl.ds(r * SHELL, SHELL), :] for r in range(row_share)]
        for k in range(col_share):
            shift = ((col_offsets[k] + GROUP - k) & (GROUP - 1)) * SHELL
            windows = [
                (pl.ds(row_starts[r], SHELL), pl.ds(col_starts[k], LANES))
                for r in range(row_share)
            ]
            inside = granule == col_offsets[k]
            sums = [
                held[windows[r]] + jnp.where(inside, pltpu.roll(slabs[r], shift, 1), 0.0)
                for r in range(row_share)
            ]
            for r in range(row_share):
                held[windows[r]] = sums[r]
        return carry

    lax.fori_loop(0, rows * cols, step, 0, unroll=2)
    copy_chunks(held, out_ref, sems)


def split_bf16(values):
    high = values.astype(jnp.bfloat16)
    return high, (values - high.astype(jnp.float32)).astype(jnp.bfloat16)


def swap_table(half_ref, stage_ref):
    for a in range(SHELL // GROUP):
        for b in range(SHELL // GROUP):
            arrays = [
                half_ref[b, pl.ds(GROUP * a + i, SHELL, stride=SHELL), :] for i in range(GROUP)
            ]
            for j, array in enumerate(swap_granules(arrays)):
                stage_ref[a, pl.ds(GROUP * b + j, SHELL, stride=SHELL), :] = array


def table_stage(classes, tables_ref, half_ref, stage_ref, tab_ref):
    width = SHELL * SHELL
    row = lax.broadcasted_iota(jnp.int32, (width, width), 0)
    column = lax.broadcasted_iota(jnp.int32, (width, width), 1)
    swap = (row // SHELL == column % SHELL) & (row % SHELL == column // SHELL)
    swap = jnp.where(swap, 1.0, 0.0).astype(jnp.bfloat16)

    def keep(klass, form, values):
        for turn, array in enumerate((values.T, values)):
            high, low = split_bf16(array)
            tab_ref[klass, form + turn, 0] = high
            tab_ref[klass, form + turn, 1] = low

    def swapped(values):
        for half in range(2):
            half_ref[half] = values[:, half * LANES : (half + 1) * LANES]
        swap_table(half_ref, stage_ref)
        return -0.5 * jnp.concatenate([stage_ref[0], stage_ref[1]], axis=1)

    def step(klass, carry):
        values = tables_ref[klass]
        keep(klass, 0, values)
        keep(klass, 2, swapped(values))
        high, low = split_bf16(values)
        permuted = jnp.dot(high, swap, preferred_element_type=jnp.float32)
        permuted = permuted + jnp.dot(low, swap, preferred_element_type=jnp.float32)
        keep(klass, 4, swapped(permuted))
        return carry

    lax.fori_loop(0, classes, step, 0)


def index_stage(classes, slots, task_count, col_share, slabs, bra, ket, klass, live, index_ref):
    a, b = bra // task_count, bra % task_count
    c, d = ket // task_count, ket % task_count

    def at(v):
        return (v % col_share) * slabs + (v // col_share) * task_count

    at_c, at_d = at(c), at(d)
    pairs = (c + at_d, a + at(b), b + at_d, a + at_c, b + at_c, a + at_d)
    for form in range(6):
        index_ref[form : form + 1, :] = 2 * pairs[form]
    lane = lax.broadcasted_iota(jnp.int32, (8, slots), 1)
    line = lax.broadcasted_iota(jnp.int32, (8, slots), 0)
    member = (jnp.broadcast_to(klass, (8, slots)) == line) & (lane < live)
    member = jnp.where(member, 1.0, 0.0)
    earlier = lax.broadcasted_iota(jnp.int32, (slots, slots), 0)
    later = lax.broadcasted_iota(jnp.int32, (slots, slots), 1)
    before = jnp.where(earlier < later, 1.0, 0.0).astype(jnp.bfloat16)
    ranks = jnp.dot(member.astype(jnp.bfloat16), before, preferred_element_type=jnp.float32)
    rank = jnp.sum(ranks * member, axis=0, keepdims=True).astype(jnp.int32)
    alive = lane[0:1] < live
    index_ref[6:7, :] = 2 * jnp.where(alive, klass * slots + rank, classes * slots)
    sizes = jnp.sum(member, axis=1, keepdims=True)
    sizes = jnp.sum(jnp.where(lane == line, sizes, 0.0), axis=0, keepdims=True)
    index_ref[7:8, :] = sizes.astype(jnp.int32)


def fetch_kernel(
    rows, cols, src_ref, tables_ref, dst_ref, tab_ref,
    half_ref, stage_ref, send_sem, recv_sem, own_sem,
):
    exchange_kernel(
        rows, cols, src_ref, dst_ref, send_sem, recv_sem, own_sem,
        lambda: table_stage(tables_ref.shape[0], tables_ref, half_ref, stage_ref, tab_ref),
    )


def pack_kernel(
    rows, cols, row_share, col_share, task_count, classes,
    place_ref, tasks_ref, count_ref, bra_ref, ket_ref, class_ref, held, out_ref, index_ref,
):
    index_stage(
        classes, bra_ref.shape[1], task_count, col_share, rows * cols * row_share,
        bra_ref[...], ket_ref[...], class_ref[...], count_ref[0], index_ref,
    )
    row_blocks, col_blocks = held.shape[0] // SHELL, held.shape[1] // SHELL
    granule = lane_granule(SHELL)

    def step(slot, carry):
        device = lax.rem(slot, rows) * cols + lax.div(slot, rows)
        row_starts, col_starts, col_offsets = places_of(
            device, place_ref, tasks_ref, row_share, col_share, row_blocks, col_blocks
        )
        slabs = [jnp.zeros((SHELL, LANES), jnp.float32)] * row_share
        for k in range(col_share):
            shift = ((k + GROUP - col_offsets[k]) & (GROUP - 1)) * SHELL
            for r in range(row_share):
                block = held[pl.ds(row_starts[r], SHELL), pl.ds(col_starts[k], LANES)]
                slabs[r] = jnp.where(granule == k, pltpu.roll(block, shift, 1), slabs[r])
        for r in range(row_share):
            out_ref[slot, pl.ds(r * SHELL, SHELL), :] = slabs[r]
        return carry

    lax.fori_loop(0, rows * cols, step, 0, unroll=2)


def quartet_kernel(
    classes, slots, task_count, col_share,
    work_ref, index_ref, factor_ref, count_ref, recv_ref, scale_ref, tab_ref, out_ref,
    own_scale, left_ref, right_ref, x_ref, g_ref, y_ref,
):
    slabs = recv_ref.shape[0] // SHELL
    tiles = slabs // 8

    def scale_step(u, carry):
        shell = work_ref[0, u]
        part = shell & (GROUP - 1)
        line = jnp.broadcast_to(scale_ref[pl.ds((shell - part) // GROUP, 1), :], (8, LANES))
        shift = ((GROUP - part) & (GROUP - 1)) * SHELL
        own_scale[pl.ds(u, 1), :] = pltpu.roll(line, shift, 1)[0:1]
        return carry

    lax.fori_loop(0, task_count, scale_step, 0, unroll=8)
    source = lax.broadcasted_iota(jnp.int32, (LANES, LANES), 0)
    lane = lax.broadcasted_iota(jnp.int32, (LANES, LANES), 1)
    for half in range(2):
        spread = jnp.where(source == lane // SHELL + GROUP * half, 1.0, 0.0)
        left_ref[half] = jnp.dot(own_scale[...], spread, precision=lax.Precision.HIGHEST)
    repeat = jnp.where(source == lane % SHELL, 1.0, 0.0)
    right_ref[...] = jnp.dot(own_scale[...], repeat, precision=lax.Precision.HIGHEST)

    def tile_place(tile):
        u = pl.multiple_of(lax.rem(tile * 8, task_count), 8)
        return u, lax.div(tile * 8, task_count) * col_share

    def pair_window(c, tile, half):
        return pl.ds(2 * (c * slabs + tile * 8) + half, 8, stride=2)

    def spread_step(tile, carry):
        u, v = tile_place(tile)
        for half in range(2):
            arrays = [
                recv_ref[pl.ds(tile * 8 * SHELL + GROUP * half + i, 8, stride=SHELL), :]
                for i in range(GROUP)
            ]
            arrays = swap_granules(arrays)
            left = left_ref[half, pl.ds(u, 8), :]
            for c in range(col_share):
                weight = left * right_ref[pl.ds(v + c, 1), :]
                x_ref[pair_window(c, tile, half), :] = arrays[c] * weight
        return carry

    lax.fori_loop(0, tiles, spread_step, 0, unroll=2)

    zero = jnp.zeros((64, LANES), jnp.float32)

    def zero_step(part, carry):
        for form in range(6):
            y_ref[form, pl.ds(pl.multiple_of(part * 64, 64), 64), :] = zero
        return carry

    lax.fori_loop(0, y_ref.shape[1] // 64, zero_step, 0)
    live = count_ref[0]
    batch = 4 if slots % 4 == 0 else 1
    batches = lax.div(live + batch - 1, batch)

    def pair(n, form):
        return pl.ds(pl.multiple_of(index_ref[form, n], 2), 2)

    def gather_step(step, carry):
        numbers = [step * batch + i for i in range(batch)]
        values = [[x_ref[pair(n, form), :] for form in range(6)] for n in numbers]
        for n, lines in zip(numbers, values):
            for form in range(6):
                g_ref[form, pair(n, 6), :] = lines[form]
        return carry

    lax.fori_loop(0, batches, gather_step, 0)

    def class_step(klass, carry):
        def chunk_step(chunk, carry):
            start = 2 * (klass * slots + chunk * CHUNK)
            windows = [pl.ds(start + half, CHUNK, stride=2) for half in range(2)]
            for form in range(6):
                values = jnp.concatenate([g_ref[form, window, :] for window in windows], axis=1)
                high, low = split_bf16(values)
                product = functools.partial(jnp.dot, preferred_element_type=jnp.float32)
                table_high = tab_ref[klass, form, 0]
                result = product(high, table_high) + product(low, table_high)
                result = result + product(high, tab_ref[klass, form, 1])
                for half in range(2):
                    g_ref[form, windows[half], :] = result[:, half * LANES : (half + 1) * LANES]
            return carry

        return lax.fori_loop(0, lax.div(index_ref[7, klass] + CHUNK - 1, CHUNK), chunk_step, carry)

    lax.fori_loop(0, classes, class_step, 0)

    def scatter_step(step, carry):
        numbers = [step * batch + i for i in range(batch)]
        terms = []
        for n in numbers:
            factor = jnp.where(n < live, factor_ref[0, n], 0.0)
            terms.append([g_ref[form, pair(n, 6), :] * factor for form in range(6)])
        for n, lines in zip(numbers, terms):
            targets = [pair(n, form ^ 1) for form in range(6)]
            sums = [y_ref[form, targets[form], :] + lines[form] for form in range(6)]
            for form in range(6):
                y_ref[form, targets[form], :] = sums[form]
        return carry

    lax.fori_loop(0, batches, scatter_step, 0)

    def collect_step(tile, carry):
        u, v = tile_place(tile)
        for half in range(2):
            left = left_ref[half, pl.ds(u, 8), :]
            arrays = []
            for c in range(GROUP):
                if c < col_share:
                    window = pair_window(c, tile, half)
                    total = y_ref[0, window, :]
                    for form in range(1, 6):
                        total = total + y_ref[form, window, :]
                    arrays.append(total * (left * right_ref[pl.ds(v + c, 1), :]))
                else:
                    arrays.append(jnp.zeros((8, LANES), jnp.float32))
            for i, array in enumerate(swap_granules(arrays)):
                out_ref[pl.ds(tile * 8 * SHELL + GROUP * half + i, 8, stride=SHELL), :] = array
        return carry

    lax.fori_loop(0, tiles, collect_step, 0, unroll=2)


def on_device(
    density,
    core_hamiltonian,
    class_tables,
    shell_scale,
    block_place,
    work_blocks,
    quartet_bra,
    quartet_ket,
    quartet_class,
    quartet_factor,
    quartet_count,
):
    rows = lax.axis_size("row")
    cols = lax.axis_size("col")
    count = rows * cols
    task_count = work_blocks.shape[1]
    row_share = task_count // rows
    col_share = task_count // cols
    classes = class_tables.shape[0]
    width = class_tables.shape[1]
    slots = quartet_bra.shape[1]
    message = (row_share * SHELL, LANES)
    messages = jax.ShapeDtypeStruct((count,) + message, jnp.float32)
    slab_rows = count * row_share * SHELL
    pair_rows = task_count * task_count

    vmem = pl.BlockSpec(memory_space=pltpu.VMEM)
    smem = pl.BlockSpec(memory_space=pltpu.SMEM)
    hbm = pl.BlockSpec(memory_space=pl.ANY)
    local = pltpu.CompilerParams(vmem_limit_bytes=VMEM_LIMIT)
    parts = 8

    def talk(collective_id, limit):
        return pltpu.CompilerParams(
            collective_id=collective_id, has_side_effects=True, vmem_limit_bytes=limit
        )

    def exchange(collective_id, name, values):
        return pl.pallas_call(
            functools.partial(exchange_kernel, rows, cols),
            out_shape=messages,
            in_specs=[hbm],
            out_specs=hbm,
            scratch_shapes=[
                pltpu.SemaphoreType.DMA((count,)),
                pltpu.SemaphoreType.DMA((count,)),
                pltpu.SemaphoreType.DMA,
            ],
            compiler_params=talk(collective_id, SMALL_LIMIT),
            name=name,
        )(values)

    sizes = (rows, cols, row_share, col_share)
    table_shape = (classes, 6, 2, width, width)
    tasks = pl.pallas_call(
        functools.partial(share_kernel, rows, cols, task_count),
        out_shape=jax.ShapeDtypeStruct((count, 1, LANES), jnp.int32),
        in_specs=[vmem],
        out_specs=vmem,
        scratch_shapes=[
            pltpu.VMEM((1, LANES), jnp.int32),
            pltpu.SemaphoreType.DMA((count,)),
            pltpu.SemaphoreType.DMA((count,)),
        ],
        compiler_params=talk(0, SMALL_LIMIT),
        name="share_tasks",
    )(work_blocks)
    picked, index = pl.pallas_call(
        functools.partial(pack_kernel, *sizes, task_count, classes),
        out_shape=(messages, jax.ShapeDtypeStruct((8, slots), jnp.int32)),
        in_specs=[smem] * 3 + [vmem] * 4,
        out_specs=(vmem, vmem),
        compiler_params=pltpu.CompilerParams(vmem_limit_bytes=PACK_LIMIT),
        name="pack_density",
    )(
        block_place, tasks, quartet_count, quartet_bra, quartet_ket, quartet_class, density
    )
    fetched, tables = pl.pallas_call(
        functools.partial(fetch_kernel, rows, cols),
        out_shape=(messages, jax.ShapeDtypeStruct(table_shape, jnp.bfloat16)),
        in_specs=[hbm, vmem],
        out_specs=(hbm, vmem),
        scratch_shapes=[
            pltpu.VMEM((2, width, LANES), jnp.float32),
            pltpu.VMEM((2, width, LANES), jnp.float32),
            pltpu.SemaphoreType.DMA((count,)),
            pltpu.SemaphoreType.DMA((count,)),
            pltpu.SemaphoreType.DMA,
        ],
        compiler_params=talk(1, PACK_LIMIT),
        name="fetch_density",
    )(picked, class_tables)

    terms = pl.pallas_call(
        functools.partial(quartet_kernel, classes, slots, task_count, col_share),
        out_shape=jax.ShapeDtypeStruct((slab_rows, LANES), jnp.float32),
        in_specs=[smem] * 4 + [vmem] * 3,
        out_specs=vmem,
        scratch_shapes=[
            pltpu.VMEM((task_count, LANES), jnp.float32),
            pltpu.VMEM((2, task_count, LANES), jnp.float32),
            pltpu.VMEM((task_count, LANES), jnp.float32),
            pltpu.VMEM((2 * pair_rows, LANES), jnp.float32),
            pltpu.VMEM((6, 2 * (classes * slots + CHUNK), LANES), jnp.float32),
            pltpu.VMEM((6, 2 * pair_rows, LANES), jnp.float32),
        ],
        compiler_params=pltpu.CompilerParams(vmem_limit_bytes=QUARTET_LIMIT),
        name="quartets",
    )(
        work_blocks, index, quartet_factor, quartet_count,
        fetched.reshape(slab_rows, LANES), shell_scale.reshape(-1, LANES), tables,
    )
    returned = exchange(2, "return_fock", terms.reshape(messages.shape))

    return pl.pallas_call(
        functools.partial(place_kernel, *sizes),
        out_shape=jax.ShapeDtypeStruct(density.shape, jnp.float32),
        in_specs=[smem, smem, vmem, hbm],
        out_specs=hbm,
        scratch_shapes=[
            pltpu.VMEM(density.shape, jnp.float32),
            pltpu.SemaphoreType.DMA((parts,)),
        ],
        compiler_params=local,
        name="place_fock",
    )(block_place, tasks, returned, core_hamiltonian)


def solution(mesh):
    placed = (
        P("row", "col"),
        P("row", "col"),
        P(),
        P(),
        P(),
        P(("row", "col"), None),
        P(("row", "col"), None),
        P(("row", "col"), None),
        P(("row", "col"), None),
        P(("row", "col"), None),
        P(("row", "col")),
    )
    return jax.shard_map(
        on_device, mesh=mesh, in_specs=placed, out_specs=P("row", "col"), check_vma=False
    )
```
